512 devices in a mesh: ctx: 16 (over y, x), tp: 8 (over z_lo, core), dp: 4 (over z_hi).
Axes of the slice: x: 4, y: 4, z: 16 (z_hi: 4, z_lo: 4; z = z_hi * 4 + z_lo), core: 2. Of those that a mesh axis runs over, the one named last changes fastest.
Arguments:
- queries: bfloat16 [8192, 8192], P(('dp', 'ctx'), 'tp'), parts along dimension 0
- key_rows: bfloat16 [8192, 1024], P(('dp', 'ctx'), 'tp'), parts along dimension 0
- value_rows: bfloat16 [8192, 1024], P(('dp', 'ctx'), 'tp'), parts along dimension 0, may hold values from -6 to 6
- doc_lengths: int32 [32], P('dp'), parts along dimension 0, may hold values from 1 to 1024, 2048 in all
- unit_source: int32 [1024], P('dp'), parts along dimension 0, may hold values from 0 to 255, as said below
- w_out: bfloat16 [8192, 16384], P('tp', 'ctx'), may hold values from -0.0625 to 0.0625
Outputs:
- projected: bfloat16 [8192, 16384], P(('dp', 'tp'), 'ctx'), parts along dimension 0
The draws below stay inside these ranges and needn't reach their ends.
There are 4 independent parts, one for each index of `dp`. The reference program is written for one: setup_inputs(seed, part) draws one part's arguments, and reference() takes and returns one part's arrays. A program takes and returns all parts, laid end to end along the dimension named above; an argument that names none is the same for every part. Nothing has to cross between parts.
Inputs may be any that keep to these rules, and one draw needn't show every extreme that they name: `unit_source`: each run of 16 slots (one device's units in the balanced order) holds exactly one unit from every run of 16 units of the packed order; every unit appears once. `doc_lengths`: they sum to 2048; the longest is exactly 1024.
All inputs are finite; a program needn't handle non-finite values.
Results may differ from the reference program's by a relative error of at most 0.017.
Values may be sent and summed in bfloat16 or wider, within the bound.
A program may use at most 64 MiB of HBM per device.

```python
import math
import jax
import jax.numpy as jnp
import numpy as np
from jax import lax

D = 16384
HQ = 64
KVH = 8
HD = 128
DOCS = 8
TOKENS = 2048
UNITS = 256
MOSTLEN = 1024
HEAD_BLOCKS = 8
N_CTX = 16


def drawn_rows(key):
    key_first = jax.random.fold_in(key, 0)
    shared_base = jax.random.normal(key_first, (TOKENS, KVH * HD), jnp.float32)
    return shared_base


def draw_key_rows(key, part):
    shared_base = drawn_rows(key)
    drawn = shared_base
    return drawn.astype(jnp.bfloat16)


def draw_queries(key, part):
    key = jax.random.fold_in(key, 22)
    key_first = jax.random.fold_in(key, 0)
    result = jax.random.normal(key_first, (TOKENS, HQ * HD), jnp.float32)
    return result.astype(jnp.bfloat16)


def draw_unit_source(key, part):
    key = jax.random.fold_in(key, 23)
    key_first, second = jax.random.split(key)
    device_count = N_CTX
    orders = jax.vmap(lambda subkey: jax.random.permutation(subkey, device_count))(jax.random.split(key_first, device_count))
    unit_order = jax.vmap(lambda subkey: jax.random.permutation(subkey, device_count))(jax.random.split(second, device_count))
    dest_grid = jnp.broadcast_to(jnp.arange(device_count)[:, None], (device_count, device_count))
    within = unit_order[orders, dest_grid]
    return (orders * device_count + within).reshape(device_count * device_count).astype(jnp.int32)


def shard_levels(own_key, shape, cuts, smallest, largest):
    level, own = 1.0, jax.random.fold_in(own_key, 6)
    for position, blocks in cuts:
        heights = jnp.exp(jax.random.uniform(jax.random.fold_in(own, position), (blocks,), jnp.float32, smallest / len(cuts), largest / len(cuts)))
        level = level * jnp.repeat(heights, shape[position] // blocks).reshape([-1 if axis == position else 1 for axis in range(len(shape))])
    return level


def length_profile(amount, total, limit, lean):
    portions = [(1 << 20) // math.isqrt(rank ** lean) + 1 for rank in range(2, amount + 1)]
    spare, given = total - limit - (amount - 1), [1] * (amount - 1)
    while spare > 0:
        candidates = [i for i in range(amount - 1) if given[i] < limit]
        mass, remaining = sum([portions[i] for i in candidates]), spare
        for i in candidates:
            more = min(limit - given[i], max(1, remaining * portions[i] // mass), spare)
            given[i] = given[i] + more
            spare = spare - more
    return np.array([limit] + given)


def uneven(stream_key, amount, total, reach, lean):
    if amount == 2:
        one = jax.random.randint(stream_key, (), max(1, total - reach), min(reach, total - 1) + 1)
        return jnp.stack([one, total - one])
    tallies = jnp.asarray(length_profile(amount, total, reach, lean), jnp.int32)
    pairs = (amount - 1) // 2
    source_of, sink = tallies[1:1 + 2 * pairs:2], tallies[2:2 + 2 * pairs:2]
    slack = jnp.minimum(source_of - 1, reach - sink)
    shifted = jax.random.randint(jax.random.fold_in(stream_key, 1), (pairs,), 0, 1 << 20) % (slack + 1)
    tallies = tallies.at[1:1 + 2 * pairs:2].set(source_of - shifted).at[2:2 + 2 * pairs:2].set(sink + shifted)
    return tallies[jax.random.permutation(jax.random.fold_in(stream_key, 2), amount)]


def normal_values(stream_key, dims, width, most, cuts=(), held_as=jnp.bfloat16):
    array = width * jax.random.normal(stream_key, dims, jnp.float32)
    if cuts:
        array = array * shard_levels(stream_key, dims, cuts, -0.22, 0.18)
    return jnp.clip(array, -most, most).astype(held_as)


def setup_inputs(seed: int = 0, part: int = 0) -> dict:
    streams_of = jax.random.split(jax.random.key(seed), 7)
    own_keys = jax.random.split(jax.random.fold_in(streams_of[6], part), 7)
    return {
        "queries": draw_queries(jax.random.fold_in(jax.random.fold_in(streams_of[6], part), 71), part),
        "key_rows": draw_key_rows(jax.random.fold_in(jax.random.fold_in(streams_of[6], part), 71), part),
        "value_rows": normal_values(own_keys[2], (TOKENS, KVH * HD), 1.0, 6.0, ((0, 16), (1, 8))),
        "doc_lengths": uneven(own_keys[3], DOCS, TOKENS, MOSTLEN, 2).astype(jnp.int32),
        "unit_source": draw_unit_source(jax.random.fold_in(jax.random.fold_in(streams_of[6], part), 71), part),
        "w_out": normal_values(streams_of[5], (HQ * HD, D), (HQ * HD) ** -0.5, 0.0625, ((0, 8), (1, 16))),
    }


def doc_index(positions, doc_ends):
    return jnp.sum((positions[None, :] >= doc_ends[:, None]).astype(jnp.int32), axis=0)


def reference(queries, key_rows, value_rows, doc_lengths, unit_source, w_out):
    group_size = HQ // KVH
    doc_ends = jnp.cumsum(doc_lengths).astype(jnp.int32)
    positions = jnp.arange(TOKENS, dtype=jnp.int32)
    token_doc = doc_index(positions, doc_ends)
    visible = (token_doc[:, None] == token_doc[None, :]) & (positions[None, :] <= positions[:, None])
    query_heads = queries.reshape(TOKENS, KVH, group_size, HD).transpose(1, 0, 2, 3)
    key_heads = key_rows.reshape(TOKENS, KVH, HD).transpose(1, 0, 2)
    value_heads = value_rows.reshape(TOKENS, KVH, HD).transpose(1, 0, 2)

    def one_group(operands):
        query_group, key_group, value_group = operands
        scores = jnp.einsum("tgd,sd->gts", query_group.astype(jnp.float32), key_group.astype(jnp.float32)) * (HD ** -0.5)
        scores = jnp.where(visible[None], scores, -jnp.inf)
        row_max = jnp.max(scores, axis=2, keepdims=True)
        weights = jnp.where(visible[None], jnp.exp(scores - row_max), 0.0)
        totals = jnp.sum(weights, axis=2)
        rounded = lax.optimization_barrier(weights.astype(jnp.bfloat16))
        blended = jnp.einsum("gts,sd->gtd", rounded.astype(jnp.float32), value_group.astype(jnp.float32))
        return (blended / totals[..., None]).astype(jnp.bfloat16)

    attended = lax.map(one_group, (query_heads, key_heads, value_heads))
    attended = attended.transpose(2, 0, 1, 3).reshape(TOKENS, HQ * HD)
    unit_rows = TOKENS // UNITS
    source_rows = (unit_source[:, None] * unit_rows + jnp.arange(unit_rows, dtype=jnp.int32)[None, :]).reshape(TOKENS)
    balanced = jnp.take(attended, source_rows, axis=0)
    block_cols = HQ * HD // HEAD_BLOCKS
    running_total = jnp.zeros((TOKENS, D), jnp.float32)
    for block_index in range(HEAD_BLOCKS):
        lower = block_index * block_cols
        partial_value = jnp.dot(balanced[:, lower:lower + block_cols], w_out[lower:lower + block_cols], preferred_element_type=jnp.float32)
        running_total = running_total + lax.optimization_barrier(partial_value.astype(jnp.bfloat16)).astype(jnp.float32)
    return running_total.astype(jnp.bfloat16)
```

```python
import functools

import jax
import jax.numpy as jnp
from jax import lax
from jax.experimental import pallas as pl
from jax.experimental.pallas import tpu as pltpu
from jax.sharding import PartitionSpec as P

HD = 128
UNIT = 8
SPAN = 9
MESH = pl.DeviceIdType.MESH


def kernel(
    lengths_ref, units_ref, q_ref, k_ref, v_ref, w_ref, out_ref,
    kv_buf, slots, w_buf, q_in, order, out_order, q_heads, pos_buf, bias, k_cat, v_cat, att,
    part_out, part_in,
    load_sem, w_send, w_recv, kv_send, kv_recv, ag_send, ag_recv,
    give_send, give_recv, rs_send, rs_recv,
):
    ctx, tp, dp = lax.axis_index("ctx"), lax.axis_index("tp"), lax.axis_index("dp")
    y, x = ctx // 4, ctx % 4
    zl, core = tp // 2, tp % 2
    sign = 1 - 2 * core

    def at_plane(yy, xx):
        return {"ctx": ((yy + 4) % 4) * 4 + (xx + 4) % 4}

    def at_z(step):
        moved = zl + step + 4
        return {"tp": (moved % 4) * 2 + core, "dp": (dp + moved // 4 + 3) % 4}

    def at_part(step, c):
        return {"tp": zl * 2 + c, "dp": (dp + step + 4) % 4}

    x_next, x_prev = at_plane(y, x + 1), at_plane(y, x - 1)
    y_next, y_prev = at_plane(y + 1, x), at_plane(y - 1, x)
    twin = {"tp": zl * 2 + 1 - core}

    loads = [
        pltpu.make_async_copy(k_ref, kv_buf.at[0, y, x], load_sem.at[0]),
        pltpu.make_async_copy(v_ref, kv_buf.at[1, x, y], load_sem.at[1]),
        pltpu.make_async_copy(q_ref, q_in, load_sem.at[2]),
        pltpu.make_async_copy(w_ref, w_buf.at[core], load_sem.at[3]),
    ]
    for load in loads:
        load.start()

    barrier = pltpu.get_barrier_semaphore()
    partners = [
        x_next, x_prev, y_next, y_prev, twin, at_z(1), at_z(-1),
        at_part(1, core), at_part(-1, core), at_part(1, 1 - core), at_part(-1, 1 - core),
    ]
    for partner in partners:
        pl.semaphore_signal(barrier, inc=1, device_id=partner, device_id_type=MESH)
    pl.semaphore_wait(barrier, len(partners))

    def gather_copies(buf, send, recv):
        copies = {}
        for half in range(2):
            first, second = (x, y) if half == 0 else (y, x)
            first_to = (x_next, x_prev) if half == 0 else (y_next, y_prev)
            second_to = (y_next, y_prev) if half == 0 else (x_next, x_prev)
            for way in range(2):
                back = 3 if way == 0 else 1
                regions = (
                    (buf.at[half, second, first], first_to[way]),
                    (buf.at[half, second, (first + back) % 4, way], first_to[way]),
                    (buf.at[half, second], second_to[way]),
                    (buf.at[half, (second + back) % 4, :, way], second_to[way]),
                )
                for stage, (region, target) in enumerate(regions):
                    copies[half, stage, way] = pltpu.make_async_remote_copy(
                        src_ref=region,
                        dst_ref=region,
                        send_sem=send.at[half, stage, way],
                        recv_sem=recv.at[half, stage, way],
                        device_id=target,
                        device_id_type=MESH,
                    )
        return copies

    def begin(copies, stage):
        for way in range(2):
            for half in range(2):
                copies[half, stage, way].start()

    def arrive(copies, stage):
        for way in range(2):
            for half in range(2):
                copies[half, stage, way].wait_recv()

    def sent(copies):
        for copy in copies.values():
            copy.wait_send()

    kv = gather_copies(kv_buf, kv_send, kv_recv)
    loads[0].wait()
    loads[1].wait()
    begin(kv, 0)
    w_copy = pltpu.make_async_remote_copy(
        src_ref=w_ref, dst_ref=w_buf.at[core], send_sem=w_send, recv_sem=w_recv,
        device_id=twin, device_id_type=MESH,
    )
    w_copy.start()
    arrive(kv, 0)
    begin(kv, 1)

    row8 = lax.broadcasted_iota(jnp.int32, (UNIT, HD), 0)
    lane8 = lax.broadcasted_iota(jnp.int32, (UNIT, HD), 1)

    def place(d, carry):
        unit = jnp.zeros((UNIT, HD), jnp.int32)
        for i in range(16):
            value = jnp.full((UNIT, HD), units_ref[d * 16 + i])
            unit = jnp.where(lax.shift_right_logical(value, 4) == ctx, value & 15, unit)
        row = unit * UNIT + row8
        rows = pl.ds(pl.multiple_of(d * UNIT, UNIT), UNIT)
        pos_buf[rows, :] = ctx * 128 + row
        order[rows, :] = (lane8 == row).astype(jnp.float32)
        return carry

    lax.fori_loop(0, 16, place, 0)
    for n in range(32):
        value = jnp.full((UNIT, HD), units_ref[tp * 32 + n])
        row = lax.shift_right_logical(value, 4) * 16 + (n // 16) * UNIT + row8
        for side in range(2):
            out_order[n * UNIT:(n + 1) * UNIT, side * HD:(side + 1) * HD] = (
                lane8 + side * HD == row
            ).astype(jnp.float32)
    arrive(kv, 1)
    begin(kv, 2)
    loads[2].wait()
    ordered = jnp.dot(
        order[...].astype(jnp.bfloat16), q_in[...], preferred_element_type=jnp.float32
    ).astype(jnp.bfloat16)
    for head in range(8):
        q_heads[head] = ordered[:, head * HD:(head + 1) * HD]
    pos = pos_buf[...]
    begins = jnp.zeros_like(pos)
    end = jnp.int32(0)
    for j in range(8):
        end = end + lengths_ref[j]
        begins = jnp.where(pos >= end, end, begins)
    lane = lax.broadcasted_iota(jnp.int32, (128, HD), 1)
    for block in range(SPAN):
        key_pos = (ctx - (SPAN - 1) + block) * 128 + lane
        seen = (key_pos >= begins) & (key_pos <= pos)
        bias[:, block * 128:(block + 1) * 128] = jnp.where(seen, 0.0, -1e30)
    v_cat[:, HD:] = jnp.ones((SPAN * 128, HD), jnp.bfloat16)
    arrive(kv, 2)
    begin(kv, 3)
    arrive(kv, 3)
    for block in range(SPAN):
        other = (ctx + 16 - (SPAN - 1) + block) % 16
        oy, ox = other // 4, other % 4
        for part in range(2):
            rows = slice(block * 128 + part * 64, block * 128 + part * 64 + 64)
            k_cat[rows, :] = kv_buf[0, oy, ox, part]
            v_cat[rows, :HD] = kv_buf[1, ox, oy, part]

    factor = (HD ** -0.5) * 1.4426950408889634
    for pair in range(4):
        two = jnp.concatenate([q_heads[2 * pair], q_heads[2 * pair + 1]], axis=0)
        scores = lax.dot_general(
            two, k_cat[...], (((1,), (1,)), ((), ())),
            preferred_element_type=jnp.float32,
        )
        masked = jnp.concatenate([scores[:128] + bias[...], scores[128:] + bias[...]], axis=0)
        top = jnp.max(masked, axis=1, keepdims=True)
        weights = jnp.exp2((masked - top) * factor).astype(jnp.bfloat16)
        blended = jnp.dot(weights, v_cat[...], preferred_element_type=jnp.float32)
        result = (blended[:, :HD] / blended[:, HD:]).astype(jnp.bfloat16)
        for one in range(2):
            head = 2 * pair + one
            col = (head % 4) * HD
            att[:, head // 4, :, col:col + HD] = result[one * 128:(one + 1) * 128].reshape(8, 16, HD)

    def chunk_step(k, s):
        return (-s, 2 * s, s, 0 * s)[k]

    def give(k, c):
        s = 1 - 2 * c
        shifted = zl + chunk_step(k, s) + 4
        block = shifted % 4
        ahead = 1 - shifted // 4
        return att.at[2 * block + c], ahead

    given, kept, gone = {}, {}, {}
    halves = (slots.at[:, 0, y, x], slots.at[:, 1, x, y])

    def slot(k, half_is_core_one):
        return slots.at[k, 1, x, y] if half_is_core_one else slots.at[k, 0, y, x]

    def both(emit):
        for c in range(2):
            pl.when(core == c)(functools.partial(emit, c))

    def start_gifts(k, c):
        rows, ahead = give(k, 1 - c)
        pltpu.make_async_remote_copy(
            src_ref=rows, dst_ref=slot(k, c == 1), send_sem=give_send.at[k, 1],
            recv_sem=give_recv.at[k, c], device_id=at_part(ahead, 1 - c), device_id_type=MESH,
        ).start()
        rows, ahead = give(k, c)

        @pl.when(ahead == 0)
        def _():
            pltpu.make_async_copy(rows, slot(k, c == 1), give_recv.at[k, c]).start()

        @pl.when(ahead != 0)
        def _():
            pltpu.make_async_remote_copy(
                src_ref=rows, dst_ref=slot(k, c == 1), send_sem=give_send.at[k, 0],
                recv_sem=give_recv.at[k, c], device_id=at_part(ahead, c), device_id_type=MESH,
            ).start()

    def end_gifts(k, c):
        rows, ahead = give(k, c)
        pltpu.make_async_copy(rows, rows, give_send.at[k, 1]).wait()

        @pl.when(ahead != 0)
        def _():
            pltpu.make_async_copy(rows, rows, give_send.at[k, 0]).wait()

    def gifts_in(k):
        for half in range(2):
            pltpu.make_async_copy(att.at[0], slot(k, half == 1), give_recv.at[k, half]).wait()

    for k in range(4):
        both(functools.partial(start_gifts, k))

    gathers = [gather_copies(slots.at[k], ag_send.at[k], ag_recv.at[k]) for k in range(4)]

    def s1(k):
        gifts_in(k)
        begin(gathers[k], 0)

    def s2(k):
        arrive(gathers[k], 0)
        begin(gathers[k], 1)

    def s3(k):
        arrive(gathers[k], 1)
        begin(gathers[k], 2)

    def s4(k):
        arrive(gathers[k], 2)
        begin(gathers[k], 3)

    def hand_on(k, j):
        step = (-sign, sign, sign)[k]
        return pltpu.make_async_remote_copy(
            src_ref=part_out.at[k, j], dst_ref=part_in.at[k, j],
            send_sem=rs_send.at[k, j], recv_sem=rs_recv.at[k, j],
            device_id=at_z(step), device_id_type=MESH,
        )

    def project(k):
        arrive(gathers[k], 3)

        def tile(j, carry):
            cols = pl.ds(pl.multiple_of(j * 256, 256), 256)
            acc = jnp.zeros((256, 256), jnp.float32)
            for half in range(2):
                for part in range(2):
                    left = jnp.concatenate(
                        [
                            slots[k, half, a, b, part]
                            for a, b in (
                                (n // 4, n % 4) if half == 0 else (n % 4, n // 4) for n in range(16)
                            )
                        ],
                        axis=0,
                    )
                    acc = acc + jnp.dot(
                        left, w_buf[half, part * 512:(part + 1) * 512, cols],
                        preferred_element_type=jnp.float32,
                    )
            if k == 2:
                hand_on(1, j).wait_recv()
                acc = acc + part_in[1, j].astype(jnp.float32)
            if k == 3:
                hand_on(0, j).wait_recv()
                hand_on(2, j).wait_recv()
                acc = acc + part_in[0, j].astype(jnp.float32) + part_in[2, j].astype(jnp.float32)
                out_ref[:, cols] = jnp.dot(
                    out_order[...].astype(jnp.bfloat16), acc.astype(jnp.bfloat16),
                    preferred_element_type=jnp.float32,
                ).astype(jnp.bfloat16)
            else:
                part_out[k, j] = acc.astype(jnp.bfloat16)
                hand_on(k, j).start()
            return carry

        lax.fori_loop(0, 4, tile, 0)

    s1(0)
    s2(0)
    s1(1)
    s3(0)
    s2(1)
    s1(2)
    s4(0)
    s3(1)
    s2(2)
    s1(3)
    w_copy.wait()
    loads[3].wait()
    project(0)
    s4(1)
    s3(2)
    s2(3)
    project(1)
    s4(2)
    s3(3)
    project(2)
    s4(3)
    sent(kv)
    for k in range(4):
        both(functools.partial(end_gifts, k))
    for k in range(3):
        sent(gathers[k])
    project(3)

    sent(gathers[3])
    for k in range(3):
        for j in range(4):
            hand_on(k, j).wait_send()


def local(queries, key_rows, value_rows, doc_lengths, unit_source, w_out):
    bf16, f32, i32 = jnp.bfloat16, jnp.float32, jnp.int32
    dma = pltpu.SemaphoreType.DMA
    vmem = pltpu.VMEM
    anywhere = pl.BlockSpec(memory_space=pl.ANY)
    smem = pl.BlockSpec(memory_space=pltpu.SMEM)
    return pl.pallas_call(
        kernel,
        out_shape=jax.ShapeDtypeStruct((256, 1024), bf16),
        in_specs=[smem, smem, anywhere, anywhere, anywhere, anywhere],
        out_specs=pl.BlockSpec(memory_space=pltpu.VMEM),
        scratch_shapes=[
            vmem((2, 4, 4, 2, 64, HD), bf16),
            vmem((4, 2, 4, 4, 2, 16, 512), bf16),
            vmem((2, 1024, 1024), bf16),
            vmem((128, 1024), bf16),
            vmem((128, HD), f32),
            vmem((256, 256), f32),
            vmem((8, 128, HD), bf16),
            vmem((128, HD), i32),
            vmem((128, SPAN * 128), f32),
            vmem((SPAN * 128, HD), bf16),
            vmem((SPAN * 128, 2 * HD), bf16),
            vmem((8, 2, 16, 512), bf16),
            vmem((3, 4, 256, 256), bf16),
            vmem((3, 4, 256, 256), bf16),
            dma((4,)),
            dma,
            dma,
            dma((2, 4, 2)),
            dma((2, 4, 2)),
            dma((4, 2, 4, 2)),
            dma((4, 2, 4, 2)),
            dma((4, 2)),
            dma((4, 2)),
            dma((3, 4)),
            dma((3, 4)),
        ],
        compiler_params=pltpu.CompilerParams(
            collective_id=0, has_side_effects=True, vmem_limit_bytes=44 << 20
        ),
        cost_estimate=pl.CostEstimate(
            flops=5_500_000_000, bytes_accessed=8_000_000, transcendentals=1_200_000
        ),
    )(
        doc_lengths, unit_source, queries,
        key_rows.reshape(2, 64, HD), value_rows.reshape(2, 64, HD), w_out,
    )


def solution(mesh):
    return jax.shard_map(
        local,
        mesh=mesh,
        in_specs=(
            P(("dp", "ctx"), "tp"),
            P(("dp", "ctx"), "tp"),
            P(("dp", "ctx"), "tp"),
            P("dp"),
            P("dp"),
            P("tp", "ctx"),
        ),
        out_specs=P(("dp", "tp"), "ctx"),
        check_vma=False,
    )
```

```python
import functools

import jax
import jax.numpy as jnp
from jax import lax
from jax.experimental import pallas as pl
from jax.experimental.pallas import tpu as pltpu
from jax.sharding import PartitionSpec as P

HD = 128
UNIT = 8
SPAN = 9
VMEM_BYTES = 63 << 20
PLAN = (
    ("attend", 0, 0), ("attend", 1, 0), ("a", 0, 0), ("attend", 3, 0), ("b", 0, 0), ("a", 3, 0),
    ("attend", 2, 0), ("b", 0, 1), ("b", 0, 2), ("f", 0, 0), ("b", 0, 3), ("a", 1, 0), ("b", 1, 0),
    ("b", 3, 1), ("f", 0, 1), ("f", 0, 2), ("f", 0, 3), ("b", 1, 2), ("b", 1, 1), ("b", 1, 3),
    ("a", 2, 0), ("done", 0, 0), ("mm", 0, 0), ("b", 2, 0), ("f", 1, 2), ("mm", 0, 1), ("f", 1, 1),
    ("f", 1, 0), ("mm", 0, 2), ("f", 1, 3), ("b", 2, 1), ("mm", 0, 3), ("b", 2, 2), ("b", 2, 3),
    ("f", 2, 0), ("b", 3, 2), ("b", 3, 0), ("done", 1, 0), ("mm", 1, 0), ("mm", 1, 1), ("f", 2, 1),
    ("mm", 1, 2), ("mm", 1, 3), ("f", 2, 2), ("f", 2, 3), ("f", 3, 2), ("b", 3, 3), ("f", 3, 0),
    ("done", 2, 0), ("mm", 2, 0), ("f", 3, 1), ("mm", 2, 1), ("mm", 2, 2), ("mm", 2, 3),
    ("f", 3, 3), ("done", 3, 0), ("mm", 3, 0), ("mm", 3, 1), ("mm", 3, 2), ("mm", 3, 3),
)
MESH = pl.DeviceIdType.MESH


def kernel(
    lengths_in, units_in, q_ref, k_ref, v_ref, w_ref, out_ref,
    lengths_ref, units_ref, kv_buf, slots, w_buf, q_in, order, out_order, q_rows, pos_buf,
    bias, k_cat, v_cat, att, part_out, part_in, out_tiles,
    load_sem, w_send, w_recv, kv_send, kv_recv, ag_send, ag_recv,
    give_send, give_recv, rs_send, rs_recv, out_sem,
):
    ctx, tp, dp = lax.axis_index("ctx"), lax.axis_index("tp"), lax.axis_index("dp")
    y, x = ctx // 4, ctx % 4
    zl, core = tp // 2, tp % 2
    sign = 1 - 2 * core

    def at_plane(yy, xx):
        return {"ctx": ((yy + 4) % 4) * 4 + (xx + 4) % 4}

    def at_z(step):
        moved = zl + step + 4
        return {"tp": (moved % 4) * 2 + core, "dp": (dp + moved // 4 + 3) % 4}

    def at_part(step, c):
        return {"tp": zl * 2 + c, "dp": (dp + step + 4) % 4}

    x_to = (at_plane(y, x + 1), at_plane(y, x - 1), at_plane(y, x + 2))
    y_to = (at_plane(y + 1, x), at_plane(y - 1, x), at_plane(y + 2, x))
    twin = {"tp": zl * 2 + 1 - core}

    barrier = pltpu.get_barrier_semaphore()
    partners = [
        *x_to, *y_to, twin, at_z(1), at_z(-1),
        at_part(1, core), at_part(-1, core), at_part(1, 1 - core), at_part(-1, 1 - core),
    ]
    for partner in partners:
        pl.semaphore_signal(barrier, inc=1, device_id=partner, device_id_type=MESH)

    loads = [
        pltpu.make_async_copy(k_ref, kv_buf.at[0, y, x], load_sem.at[0]),
        pltpu.make_async_copy(v_ref, kv_buf.at[1, x, y], load_sem.at[1]),
        pltpu.make_async_copy(units_in, units_ref, load_sem.at[2]),
        pltpu.make_async_copy(lengths_in, lengths_ref, load_sem.at[3]),
        pltpu.make_async_copy(q_ref, q_in, load_sem.at[4]),
        pltpu.make_async_copy(w_ref, w_buf.at[core], load_sem.at[5]),
    ]
    for load in loads:
        load.start()

    offsets = (0, 3, 1, 2)

    def gather_copies(buf, send, recv):
        copies = {}
        for half in range(2):
            first, second = (x, y) if half == 0 else (y, x)
            first_to, second_to = (x_to, y_to) if half == 0 else (y_to, x_to)
            regions = []
            for way in range(3):
                regions.append((("a", way), buf.at[half, second, first], first_to[way]))
            for way in range(2):
                line = (second + (3 if way == 0 else 1)) % 4
                for j, offset in enumerate(offsets):
                    place = (first + offset) % 4
                    regions.append((("b", way, j), buf.at[half, second, place], second_to[way]))
                    regions.append((("f", way, j), buf.at[half, line, place, way], second_to[way]))
            for n, (name, region, target) in enumerate(regions):
                copies[(half, *name)] = pltpu.make_async_remote_copy(
                    src_ref=region, dst_ref=region, send_sem=send.at[half, n],
                    recv_sem=recv.at[half, n], device_id=target, device_id_type=MESH,
                )
        return copies

    def e0(g):
        for half in range(2):
            for way in range(2):
                g[half, "a", way].start()
        for half in range(2):
            g[half, "a", 2].start()

    def begin_b(g):
        for half in range(2):
            for way in range(2):
                g[half, "b", way, 0].start()

    def spread(g, way_in, j):
        for half in range(2):
            g[half, "a", way_in].wait_recv()
            for way in range(2):
                g[half, "b", way, j].start()

    def forward(g, j):
        for half in range(2):
            for way in range(2):
                g[half, "b", way, j].wait_recv()
                g[half, "f", way, j].start()

    def e1(g):
        spread(g, 0, 1)
        spread(g, 1, 2)
        forward(g, 0)

    def e2(g):
        spread(g, 2, 3)

    def e3(g):
        forward(g, 1)
        forward(g, 2)

    def e4(g):
        forward(g, 3)

    def e5(g):
        for j in range(4):
            for half in range(2):
                for way in range(2):
                    g[half, "f", way, j].wait_recv()

    def sent(g):
        for copy in g.values():
            copy.wait_send()

    kv = gather_copies(kv_buf, kv_send, kv_recv)
    loads[0].wait()
    loads[1].wait()
    pl.semaphore_wait(barrier, len(partners))

    e0(kv)
    begin_b(kv)
    w_copy = pltpu.make_async_remote_copy(
        src_ref=w_ref, dst_ref=w_buf.at[core], send_sem=w_send, recv_sem=w_recv,
        device_id=twin, device_id_type=MESH,
    )
    w_copy.start()
    loads[2].wait()
    loads[3].wait()

    row8 = lax.broadcasted_iota(jnp.int32, (UNIT, HD), 0)
    lane8 = lax.broadcasted_iota(jnp.int32, (UNIT, HD), 1)

    def place(d, carry):
        unit = jnp.zeros((UNIT, HD), jnp.int32)
        for i in range(16):
            value = jnp.full((UNIT, HD), units_ref[d * 16 + i])
            unit = jnp.where(lax.shift_right_logical(value, 4) == ctx, value & 15, unit)
        row = unit * UNIT + row8
        rows = pl.ds(pl.multiple_of(d * UNIT, UNIT), UNIT)
        pos_buf[rows, :] = ctx * 128 + row
        order[rows, :] = (lane8 == row).astype(jnp.float32)
        return carry

    lax.fori_loop(0, 16, place, 0)
    e1(kv)
    e2(kv)
    loads[4].wait()
    ordered = jnp.dot(
        order[...].astype(jnp.bfloat16), q_in[...], preferred_element_type=jnp.float32
    ).astype(jnp.bfloat16)
    for t in range(8):
        for head in range(8):
            q_rows[t, head * 16:(head + 1) * 16, :] = ordered[
                t * 16:(t + 1) * 16, head * HD:(head + 1) * HD
            ]
    pos = pos_buf[...]
    begins = jnp.zeros_like(pos)
    end = jnp.int32(0)
    for j in range(8):
        end = end + lengths_ref[j]
        begins = jnp.where(pos >= end, end, begins)
    lane = lax.broadcasted_iota(jnp.int32, (128, HD), 1)
    for block in range(SPAN):
        key_pos = (ctx - (SPAN - 1) + block) * 128 + lane
        seen = (key_pos >= begins) & (key_pos <= pos)
        bias[:, :, block * 128:(block + 1) * 128] = jnp.where(seen, 0.0, -1e30).reshape(8, 16, HD)
    v_cat[:, HD:] = jnp.ones((SPAN * 128, HD), jnp.bfloat16)
    e3(kv)
    e4(kv)
    for n in range(32):
        value = jnp.full((UNIT, HD), units_ref[tp * 32 + n])
        row = lax.shift_right_logical(value, 4) * 16 + (n // 16) * UNIT + row8
        for side in range(2):
            out_order[n * UNIT:(n + 1) * UNIT, side * HD:(side + 1) * HD] = (
                lane8 + side * HD == row
            ).astype(jnp.float32)
    e5(kv)
    for block in range(SPAN):
        other = (ctx + 16 - (SPAN - 1) + block) % 16
        oy, ox = other // 4, other % 4
        for part in range(2):
            rows = slice(block * 128 + part * 64, block * 128 + part * 64 + 64)
            k_cat[rows, :] = kv_buf[0, oy, ox, part]
            v_cat[rows, :HD] = kv_buf[1, ox, oy, part]

    def swapped(c):
        return zl == 3 * c

    def rows_for(i, c):
        s = 1 - 2 * c
        if i < 2:
            step = jnp.where(swapped(c), (2 * s, -s)[i], (-s, 2 * s)[i])
        else:
            step = (s, 0)[i - 2]
        shifted = zl + step + 4
        return 2 * (shifted % 4) + c, 1 - shifted // 4

    factor = (HD ** -0.5) * 1.4426950408889634

    def attend(k):
        targets = [rows_for(k, c)[0] for c in (core, 1 - core)]
        two = jnp.concatenate([q_rows[t] for t in targets], axis=0)
        scores = lax.dot_general(
            two, k_cat[...], (((1,), (1,)), ((), ())), preferred_element_type=jnp.float32
        ).reshape(2, 8, 16, SPAN * 128)
        masked = jnp.concatenate(
            [scores[n:n + 1] + bias[t][None, None] for n, t in enumerate(targets)], axis=0
        ).reshape(256, SPAN * 128)
        top = jnp.max(masked, axis=1, keepdims=True)
        weights = jnp.exp2((masked - top) * factor).astype(jnp.bfloat16)
        blended = jnp.dot(weights, v_cat[...], preferred_element_type=jnp.float32)
        result = (blended[:, :HD] / blended[:, HD:]).astype(jnp.bfloat16)
        for n, t in enumerate(targets):
            for head in range(8):
                col = (head % 4) * HD
                at = n * 128 + head * 16
                att[t, head // 4, :, col:col + HD] = result[at:at + 16]

    slot_a = jnp.where(core == 0, y, x)
    slot_b = jnp.where(core == 0, x, y)

    def give_twin(k):
        t, ahead = rows_for(k, 1 - core)
        return pltpu.make_async_remote_copy(
            src_ref=att.at[t], dst_ref=slots.at[k, core, slot_a, slot_b],
            send_sem=give_send.at[k, 1], recv_sem=give_recv.at[k, core],
            device_id=at_part(ahead, 1 - core), device_id_type=MESH,
        )

    def give_part(k):
        t, ahead = rows_for(k, core)
        return ahead, pltpu.make_async_remote_copy(
            src_ref=att.at[t], dst_ref=slots.at[k, core, slot_a, slot_b],
            send_sem=give_send.at[k, 0], recv_sem=give_recv.at[k, core],
            device_id=at_part(ahead, core), device_id_type=MESH,
        )

    def give(k):
        give_twin(k).start()
        ahead, away = give_part(k)
        pl.when(ahead != 0)(away.start)

        @pl.when(ahead == 0)
        def _():
            t, _ = rows_for(k, core)
            pltpu.make_async_copy(
                att.at[t], slots.at[k, core, slot_a, slot_b], give_recv.at[k, core]
            ).start()

    def given(k):
        give_twin(k).wait_send()
        ahead, away = give_part(k)
        pl.when(ahead != 0)(away.wait_send)

    gathers = [gather_copies(slots.at[k], ag_send.at[k], ag_recv.at[k]) for k in range(4)]

    def start(k):
        for half in range(2):
            pltpu.make_async_copy(
                att.at[0], slots.at[k, half, 0, 0], give_recv.at[k, half]
            ).wait()
        e0(gathers[k])

    def hand_on(k, j):
        return pltpu.make_async_remote_copy(
            src_ref=part_out.at[k, j], dst_ref=part_in.at[k, j],
            send_sem=rs_send.at[k, j], recv_sem=rs_recv.at[k, j],
            device_id=at_z(jnp.where(k == 0, -sign, sign)), device_id_type=MESH,
        )

    def store(j):
        cols = pl.ds(pl.multiple_of(j * 256, 256), 256)
        return pltpu.make_async_copy(out_tiles.at[j], out_ref.at[:, cols], out_sem.at[j])

    def project(i, j):
        cols = slice(j * 256, (j + 1) * 256)
        acc = jnp.zeros((256, 256), jnp.float32)
        for half in range(2):
            for part in range(2):
                left = jnp.concatenate(
                    [
                        slots[i, half, a, b, part]
                        for a, b in (
                            (n // 4, n % 4) if half == 0 else (n % 4, n // 4) for n in range(16)
                        )
                    ],
                    axis=0,
                )
                acc = acc + jnp.dot(
                    left, w_buf[half, part * 512:(part + 1) * 512, cols],
                    preferred_element_type=jnp.float32,
                )
        if i == 2:
            hand_on(1, j).wait_recv()
            acc = acc + part_in[1, j].astype(jnp.float32)
        if i == 3:
            hand_on(0, j).wait_recv()
            hand_on(2, j).wait_recv()
            acc = acc + part_in[0, j].astype(jnp.float32) + part_in[2, j].astype(jnp.float32)
            out_tiles[j] = jnp.dot(
                out_order[...].astype(jnp.bfloat16), acc.astype(jnp.bfloat16),
                preferred_element_type=jnp.float32,
            ).astype(jnp.bfloat16)
            store(j).start()
        else:
            k = 2 if i == 2 else jnp.where(swapped(core), 1 - i, i)
            part_out[k, j] = acc.astype(jnp.bfloat16)
            hand_on(k, j).start()

    def step(op, i, j):
        g = gathers[i]
        if op == "attend":
            attend(i)
            give(i)
        elif op == "a":
            start(i)
        elif op == "b":
            if j == 0:
                begin_b(g)
            else:
                spread(g, j - 1, j)
        elif op == "f":
            forward(g, j)
        elif op == "done":
            e5(g)
        else:
            project(i, j)

    for op, i, j in PLAN:
        if op == "mm" and i == 0 and j == 0:
            w_copy.wait()
            loads[5].wait()
        if op == "done" and i == 3:
            sent(kv)
            for n in range(4):
                given(n)
            for n in range(2):
                sent(gathers[n])
        step(op, i, j)
    sent(gathers[2])
    sent(gathers[3])
    for k in range(3):
        for j in range(4):
            hand_on(k, j).wait_send()
    for j in range(4):
        store(j).wait()


def local(queries, key_rows, value_rows, doc_lengths, unit_source, w_out):
    bf16, f32, i32 = jnp.bfloat16, jnp.float32, jnp.int32
    dma = pltpu.SemaphoreType.DMA
    vmem = pltpu.VMEM
    anywhere = pl.BlockSpec(memory_space=pl.ANY)
    return pl.pallas_call(
        kernel,
        out_shape=jax.ShapeDtypeStruct((256, 1024), bf16),
        in_specs=[anywhere] * 6,
        out_specs=anywhere,
        scratch_shapes=[
            pltpu.SMEM((8,), i32),
            pltpu.SMEM((256,), i32),
            vmem((2, 4, 4, 2, 64, HD), bf16),
            vmem((4, 2, 4, 4, 2, 16, 512), bf16),
            vmem((2, 1024, 1024), bf16),
            vmem((128, 1024), bf16),
            vmem((128, HD), f32),
            vmem((256, 256), f32),
            vmem((8, 128, HD), bf16),
            vmem((128, HD), i32),
            vmem((8, 16, SPAN * 128), f32),
            vmem((SPAN * 128, HD), bf16),
            vmem((SPAN * 128, 2 * HD), bf16),
            vmem((8, 2, 16, 512), bf16),
            vmem((3, 4, 256, 256), bf16),
            vmem((3, 4, 256, 256), bf16),
            vmem((4, 256, 256), bf16),
            dma((6,)),
            dma,
            dma,
            dma((2, 19)),
            dma((2, 19)),
            dma((4, 2, 19)),
            dma((4, 2, 19)),
            dma((4, 2)),
            dma((4, 2)),
            dma((3, 4)),
            dma((3, 4)),
            dma((4,)),
        ],
        compiler_params=pltpu.CompilerParams(
            collective_id=0, has_side_effects=True, vmem_limit_bytes=VMEM_BYTES
        ),
        cost_estimate=pl.CostEstimate(
            flops=5_500_000_000, bytes_accessed=8_000_000, transcendentals=1_200_000
        ),
    )(
        doc_lengths, unit_source, queries,
        key_rows.reshape(2, 64, HD), value_rows.reshape(2, 64, HD), w_out,
    )


def solution(mesh):
    return jax.shard_map(
        local,
        mesh=mesh,
        in_specs=(
            P(("dp", "ctx"), "tp"),
            P(("dp", "ctx"), "tp"),
            P(("dp", "ctx"), "tp"),
            P("dp"),
            P("dp"),
            P("tp", "ctx"),
        ),
        out_specs=P(("dp", "tp"), "ctx"),
        check_vma=False,
    )
```

```python
import functools

import jax
import jax.numpy as jnp
from jax import lax
from jax.experimental import pallas as pl
from jax.experimental.pallas import tpu as pltpu
from jax.sharding import PartitionSpec as P

HD = 128
UNIT = 8
SPAN = 9
VMEM_BYTES = 63 << 20
SOURCES = (0, 1, 2, 3, 4, 5, 7, 8, 12, 13, 15, 6, 9, 10, 11, 14)
NEAR = 11
PLAN = (
    ("attend", 0, 0), ("attend", 1, 0), ("a", 0, 0), ("attend", 3, 0), ("b", 0, 0), ("a", 3, 0),
    ("b", 0, 2), ("attend", 2, 0), ("b", 0, 1), ("f", 0, 0), ("b", 0, 3), ("a", 1, 0), ("b", 1, 0),
    ("f", 0, 1), ("f", 0, 2), ("near", 0, 0), ("f", 0, 3), ("b", 1, 1), ("b", 1, 2), ("f", 1, 0),
    ("b", 1, 3), ("a", 2, 0), ("done", 0, 0), ("b", 2, 0), ("mm", 0, 0), ("f", 1, 1), ("f", 1, 2),
    ("mm", 0, 1), ("near", 1, 0), ("f", 1, 3), ("b", 2, 1), ("mm", 0, 2), ("b", 2, 2), ("f", 2, 0),
    ("b", 2, 3), ("b", 3, 3), ("done", 1, 0), ("b", 3, 0), ("mm", 1, 0), ("b", 3, 2), ("mm", 1, 1),
    ("b", 3, 1), ("mm", 1, 2), ("mm", 1, 3), ("f", 2, 1), ("f", 2, 2), ("mm", 0, 3), ("f", 2, 3),
    ("near", 2, 0), ("f", 3, 0), ("done", 2, 0), ("f", 3, 1), ("mm", 2, 0), ("mm", 2, 1),
    ("mm", 2, 2), ("f", 3, 3), ("mm", 2, 3), ("f", 3, 2), ("done", 3, 0), ("mm", 3, 0),
    ("mm", 3, 1), ("mm", 3, 2), ("mm", 3, 3),
)
MESH = pl.DeviceIdType.MESH


def kernel(
    lengths_in, units_in, q_ref, k_ref, v_ref, w_ref, out_ref,
    lengths_ref, units_ref, kv_buf, slots, w_buf, q_in, order, out_order, q_rows, pos_buf,
    bias, k_cat, v_cat, att, part_out, part_in, out_tiles,
    load_sem, w_send, w_recv, kv_send, kv_recv, ag_send, ag_recv,
    give_send, give_recv, rs_send, rs_recv, out_sem,
):
    ctx, tp, dp = lax.axis_index("ctx"), lax.axis_index("tp"), lax.axis_index("dp")
    y, x = ctx // 4, ctx % 4
    zl, core = tp // 2, tp % 2
    sign = 1 - 2 * core

    def at_plane(yy, xx):
        return {"ctx": ((yy + 4) % 4) * 4 + (xx + 4) % 4}

    def at_z(step):
        moved = zl + step + 4
        return {"tp": (moved % 4) * 2 + core, "dp": (dp + moved // 4 + 3) % 4}

    def at_part(step, c):
        return {"tp": zl * 2 + c, "dp": (dp + step + 4) % 4}

    x_to = (at_plane(y, x + 1), at_plane(y, x - 1), at_plane(y, x + 2))
    y_to = (at_plane(y + 1, x), at_plane(y - 1, x), at_plane(y + 2, x))
    twin = {"tp": zl * 2 + 1 - core}

    barrier = pltpu.get_barrier_semaphore()
    partners = [
        *x_to, *y_to, twin, at_z(1), at_z(-1),
        at_part(1, core), at_part(-1, core), at_part(1, 1 - core), at_part(-1, 1 - core),
    ]
    for partner in partners:
        pl.semaphore_signal(barrier, inc=1, device_id=partner, device_id_type=MESH)

    loads = [
        pltpu.make_async_copy(k_ref, kv_buf.at[0, y, x], load_sem.at[0]),
        pltpu.make_async_copy(v_ref, kv_buf.at[1, x, y], load_sem.at[1]),
        pltpu.make_async_copy(units_in, units_ref, load_sem.at[2]),
        pltpu.make_async_copy(lengths_in, lengths_ref, load_sem.at[3]),
        pltpu.make_async_copy(q_ref, q_in, load_sem.at[4]),
        pltpu.make_async_copy(w_ref, w_buf.at[core], load_sem.at[5]),
    ]
    for load in loads:
        load.start()

    offsets = (0, 3, 1, 2)

    def gather_copies(buf, send, recv, direct=()):
        copies = {}
        for half in range(2):
            first, second = (x, y) if half == 0 else (y, x)
            first_to, second_to = (x_to, y_to) if half == 0 else (y_to, x_to)
            regions = []
            for way in range(3):
                regions.append((("a", way), buf.at[half, second, first], first_to[way]))
            for way in range(2):
                line = (second + (3 if way == 0 else 1)) % 4
                for j, offset in enumerate(offsets):
                    place = (first + offset) % 4
                    regions.append((("b", way, j), buf.at[half, second, place], second_to[way]))
                    if j in direct:
                        if way == 0:
                            regions.append((("d", j), buf.at[half, second, place], second_to[2]))
                    else:
                        regions.append((("f", way, j), buf.at[half, line, place, way], second_to[way]))
            for n, (name, region, target) in enumerate(regions):
                copies[(half, *name)] = pltpu.make_async_remote_copy(
                    src_ref=region, dst_ref=region, send_sem=send.at[half, n],
                    recv_sem=recv.at[half, n], device_id=target, device_id_type=MESH,
                )
        return copies

    def e0(g):
        for half in range(2):
            for way in range(2):
                g[half, "a", way].start()
        for half in range(2):
            g[half, "a", 2].start()

    def begin_d(g, j):
        for half in range(2):
            if (half, "d", j) in g:
                g[half, "d", j].start()

    def begin_b(g):
        for half in range(2):
            for way in range(2):
                g[half, "b", way, 0].start()

    def spread(g, way_in, j):
        for half in range(2):
            g[half, "a", way_in].wait_recv()
            for way in range(2):
                g[half, "b", way, j].start()
        begin_d(g, j)

    def forward(g, j):
        for half in range(2):
            for way in range(2):
                g[half, "b", way, j].wait_recv()
                if (half, "f", way, j) in g:
                    g[half, "f", way, j].start()

    def e1(g):
        spread(g, 0, 1)
        spread(g, 1, 2)
        forward(g, 0)

    def e2(g):
        spread(g, 2, 3)

    def e3(g):
        forward(g, 1)
        forward(g, 2)

    def e4(g):
        forward(g, 3)

    def e5(g, wanted=range(4)):
        for name, copy in g.items():
            if (name[1] == "f" and name[3] in wanted) or (name[1] == "d" and name[2] in wanted):
                copy.wait_recv()

    def sent(g):
        for copy in g.values():
            copy.wait_send()

    kv = gather_copies(kv_buf, kv_send, kv_recv, (3,))
    loads[0].wait()
    loads[1].wait()
    pl.semaphore_wait(barrier, len(partners))

    e0(kv)
    begin_b(kv)
    w_copy = pltpu.make_async_remote_copy(
        src_ref=w_ref, dst_ref=w_buf.at[core], send_sem=w_send, recv_sem=w_recv,
        device_id=twin, device_id_type=MESH,
    )
    w_copy.start()
    loads[2].wait()
    loads[3].wait()

    row8 = lax.broadcasted_iota(jnp.int32, (UNIT, HD), 0)
    lane8 = lax.broadcasted_iota(jnp.int32, (UNIT, HD), 1)

    def place(d, carry):
        unit = jnp.zeros((UNIT, HD), jnp.int32)
        for i in range(16):
            value = jnp.full((UNIT, HD), units_ref[d * 16 + i])
            unit = jnp.where(lax.shift_right_logical(value, 4) == ctx, value & 15, unit)
        row = unit * UNIT + row8
        rows = pl.ds(pl.multiple_of(d * UNIT, UNIT), UNIT)
        pos_buf[rows, :] = ctx * 128 + row
        order[rows, :] = (lane8 == row).astype(jnp.float32)
        return carry

    lax.fori_loop(0, 16, place, 0)
    e1(kv)
    e2(kv)
    loads[4].wait()
    ordered = jnp.dot(
        order[...].astype(jnp.bfloat16), q_in[...], preferred_element_type=jnp.float32
    ).astype(jnp.bfloat16)
    for t in range(8):
        for head in range(8):
            q_rows[t, head * 16:(head + 1) * 16, :] = ordered[
                t * 16:(t + 1) * 16, head * HD:(head + 1) * HD
            ]
    pos = pos_buf[...]
    begins = jnp.zeros_like(pos)
    end = jnp.int32(0)
    for j in range(8):
        end = end + lengths_ref[j]
        begins = jnp.where(pos >= end, end, begins)
    lane = lax.broadcasted_iota(jnp.int32, (128, HD), 1)
    for block in range(SPAN):
        key_pos = (ctx - (SPAN - 1) + block) * 128 + lane
        seen = (key_pos >= begins) & (key_pos <= pos)
        bias[:, :, block * 128:(block + 1) * 128] = jnp.where(seen, 0.0, -1e30).reshape(8, 16, HD)
    v_cat[:, HD:] = jnp.ones((SPAN * 128, HD), jnp.bfloat16)
    e3(kv)
    e4(kv)

    def place_out(n, carry):
        source = lax.shift_right_logical(jnp.full((UNIT, HD), units_ref[tp * 32 + n]), 4)
        relative = ((lax.shift_right_logical(source, 2) - y) & 3) * 4 + ((source - x) & 3)
        rank = jnp.zeros((UNIT, HD), jnp.int32)
        for r in range(1, 16):
            rank = jnp.where(relative == SOURCES[r], r, rank)
        row = rank * 16 + (n // 16) * UNIT + row8
        rows = pl.ds(pl.multiple_of(n * UNIT, UNIT), UNIT)
        for side in range(2):
            out_order[rows, side * HD:(side + 1) * HD] = (
                lane8 + side * HD == row
            ).astype(jnp.float32)
        return carry

    lax.fori_loop(0, 32, place_out, 0)
    e5(kv)
    for block in range(SPAN):
        other = (ctx + 16 - (SPAN - 1) + block) % 16
        oy, ox = other // 4, other % 4
        for part in range(2):
            rows = slice(block * 128 + part * 64, block * 128 + part * 64 + 64)
            k_cat[rows, :] = kv_buf[0, oy, ox, part]
            v_cat[rows, :HD] = kv_buf[1, ox, oy, part]

    def swapped(c):
        return zl == 3 * c

    def rows_for(i, c):
        s = 1 - 2 * c
        if i < 2:
            step = jnp.where(swapped(c), (2 * s, -s)[i], (-s, 2 * s)[i])
        else:
            step = (s, 0)[i - 2]
        shifted = zl + step + 4
        return 2 * (shifted % 4) + c, 1 - shifted // 4

    factor = (HD ** -0.5) * 1.4426950408889634

    def attend(k):
        targets = [rows_for(k, c)[0] for c in (core, 1 - core)]
        two = jnp.concatenate([q_rows[t] for t in targets], axis=0)
        scores = lax.dot_general(
            two, k_cat[...], (((1,), (1,)), ((), ())), preferred_element_type=jnp.float32
        ).reshape(2, 8, 16, SPAN * 128)
        masked = jnp.concatenate(
            [scores[n:n + 1] + bias[t][None, None] for n, t in enumerate(targets)], axis=0
        ).reshape(256, SPAN * 128)
        top = jnp.max(masked, axis=1, keepdims=True)
        weights = jnp.exp2((masked - top) * factor).astype(jnp.bfloat16)
        blended = jnp.dot(weights, v_cat[...], preferred_element_type=jnp.float32)
        result = (blended[:, :HD] / blended[:, HD:]).astype(jnp.bfloat16)
        for n, t in enumerate(targets):
            for head in range(8):
                col = (head % 4) * HD
                at = n * 128 + head * 16
                att[t, head // 4, :, col:col + HD] = result[at:at + 16]

    slot_a = jnp.where(core == 0, y, x)
    slot_b = jnp.where(core == 0, x, y)

    def give_twin(k):
        t, ahead = rows_for(k, 1 - core)
        return pltpu.make_async_remote_copy(
            src_ref=att.at[t], dst_ref=slots.at[k, core, slot_a, slot_b],
            send_sem=give_send.at[k, 1], recv_sem=give_recv.at[k, core],
            device_id=at_part(ahead, 1 - core), device_id_type=MESH,
        )

    def give_part(k):
        t, ahead = rows_for(k, core)
        return ahead, pltpu.make_async_remote_copy(
            src_ref=att.at[t], dst_ref=slots.at[k, core, slot_a, slot_b],
            send_sem=give_send.at[k, 0], recv_sem=give_recv.at[k, core],
            device_id=at_part(ahead, core), device_id_type=MESH,
        )

    def give(k):
        give_twin(k).start()
        ahead, away = give_part(k)
        pl.when(ahead != 0)(away.start)

        @pl.when(ahead == 0)
        def _():
            t, _ = rows_for(k, core)
            pltpu.make_async_copy(
                att.at[t], slots.at[k, core, slot_a, slot_b], give_recv.at[k, core]
            ).start()

    def given(k):
        give_twin(k).wait_send()
        ahead, away = give_part(k)
        pl.when(ahead != 0)(away.wait_send)

    gathers = [gather_copies(slots.at[k], ag_send.at[k], ag_recv.at[k]) for k in range(4)]

    def start(k):
        for half in range(2):
            pltpu.make_async_copy(
                att.at[0], slots.at[k, half, 0, 0], give_recv.at[k, half]
            ).wait()
        e0(gathers[k])

    groups = (slice(0, NEAR * 16), slice(NEAR * 16, 256))

    def hand_on(k, j, group):
        rows = groups[group]
        return pltpu.make_async_remote_copy(
            src_ref=part_out.at[k, j, rows], dst_ref=part_in.at[k, j, rows],
            send_sem=rs_send.at[k, j, group], recv_sem=rs_recv.at[k, j, group],
            device_id=at_z(jnp.where(k == 0, -sign, sign)), device_id_type=MESH,
        )

    def store(j):
        cols = pl.ds(pl.multiple_of(j * 256, 256), 256)
        return pltpu.make_async_copy(out_tiles.at[j], out_ref.at[:, cols], out_sem.at[j])

    at_y = [(y + d) % 4 for d in range(4)]
    at_x = [(x + d) % 4 for d in range(4)]

    def product(i, j, sources):
        acc = jnp.zeros((len(sources) * 16, 256), jnp.float32)
        for half in range(2):
            for part in range(2):
                left = []
                for n in sources:
                    sy, sx = at_y[n // 4], at_x[n % 4]
                    left.append(slots[i, half, *((sy, sx) if half == 0 else (sx, sy)), part])
                acc = acc + jnp.dot(
                    jnp.concatenate(left, axis=0),
                    w_buf[half, part * 512:(part + 1) * 512, j * 256:(j + 1) * 256],
                    preferred_element_type=jnp.float32,
                )
        return acc

    def pass_on(i, j, group):
        rows = groups[group]
        acc = product(i, j, SOURCES[:NEAR] if group == 0 else SOURCES[NEAR:])
        if i == 2:
            hand_on(1, j, group).wait_recv()
            acc = acc + part_in[1, j, rows].astype(jnp.float32)
        k = 2 if i == 2 else jnp.where(swapped(core), 1 - i, i)
        part_out[k, j, rows] = acc.astype(jnp.bfloat16)
        hand_on(k, j, group).start()

    def finish(j):
        acc = product(3, j, SOURCES)
        for group in range(2):
            hand_on(0, j, group).wait_recv()
            hand_on(2, j, group).wait_recv()
        acc = acc + part_in[0, j].astype(jnp.float32) + part_in[2, j].astype(jnp.float32)
        out_tiles[j] = jnp.dot(
            out_order[...].astype(jnp.bfloat16), acc.astype(jnp.bfloat16),
            preferred_element_type=jnp.float32,
        ).astype(jnp.bfloat16)
        store(j).start()

    def step(op, i, j):
        g = gathers[i]
        if op == "attend":
            attend(i)
            give(i)
        elif op == "a":
            start(i)
        elif op == "b":
            if j == 0:
                begin_b(g)
            else:
                spread(g, j - 1, j)
        elif op == "f":
            forward(g, j)
        elif op == "near":
            e5(g, (0,))
            for n in range(4):
                pass_on(i, n, 0)
        elif op == "done":
            e5(g, range(4) if i == 3 else (1, 2, 3))
        elif i < 3:
            pass_on(i, j, 1)
        else:
            finish(j)

    for op, i, j in PLAN:
        if op == "near" and i == 0:
            w_copy.wait()
            loads[5].wait()
        if op == "done" and i == 3:
            sent(kv)
            for n in range(4):
                given(n)
            for n in range(2):
                sent(gathers[n])
        step(op, i, j)
    sent(gathers[2])
    sent(gathers[3])
    for k in range(3):
        for j in range(4):
            hand_on(k, j, 0).wait_send()
            hand_on(k, j, 1).wait_send()
    for j in range(4):
        store(j).wait()


def local(queries, key_rows, value_rows, doc_lengths, unit_source, w_out):
    bf16, f32, i32 = jnp.bfloat16, jnp.float32, jnp.int32
    dma = pltpu.SemaphoreType.DMA
    vmem = pltpu.VMEM
    anywhere = pl.BlockSpec(memory_space=pl.ANY)
    return pl.pallas_call(
        kernel,
        out_shape=jax.ShapeDtypeStruct((256, 1024), bf16),
        in_specs=[anywhere] * 6,
        out_specs=anywhere,
        scratch_shapes=[
            pltpu.SMEM((8,), i32),
            pltpu.SMEM((256,), i32),
            vmem((2, 4, 4, 2, 64, HD), bf16),
            vmem((4, 2, 4, 4, 2, 16, 512), bf16),
            vmem((2, 1024, 1024), bf16),
            vmem((128, 1024), bf16),
            vmem((128, HD), f32),
            vmem((256, 256), f32),
            vmem((8, 128, HD), bf16),
            vmem((128, HD), i32),
            vmem((8, 16, SPAN * 128), f32),
            vmem((SPAN * 128, HD), bf16),
            vmem((SPAN * 128, 2 * HD), bf16),
            vmem((8, 2, 16, 512), bf16),
            vmem((3, 4, 256, 256), bf16),
            vmem((3, 4, 256, 256), bf16),
            vmem((4, 256, 256), bf16),
            dma((6,)),
            dma,
            dma,
            dma((2, 19)),
            dma((2, 19)),
            dma((4, 2, 19)),
            dma((4, 2, 19)),
            dma((4, 2)),
            dma((4, 2)),
            dma((3, 4, 2)),
            dma((3, 4, 2)),
            dma((4,)),
        ],
        compiler_params=pltpu.CompilerParams(
            collective_id=0, has_side_effects=True, vmem_limit_bytes=VMEM_BYTES
        ),
        cost_estimate=pl.CostEstimate(
            flops=5_500_000_000, bytes_accessed=8_000_000, transcendentals=1_200_000
        ),
    )(
        doc_lengths, unit_source, queries,
        key_rows.reshape(2, 64, HD), value_rows.reshape(2, 64, HD), w_out,
    )


def solution(mesh):
    return jax.shard_map(
        local,
        mesh=mesh,
        in_specs=(
            P(("dp", "ctx"), "tp"),
            P(("dp", "ctx"), "tp"),
            P(("dp", "ctx"), "tp"),
            P("dp"),
            P("dp"),
            P("tp", "ctx"),
        ),
        out_specs=P(("dp", "tp"), "ctx"),
        check_vma=False,
    )
```

```python
import functools

import jax
import jax.numpy as jnp
from jax import lax
from jax.experimental import pallas as pl
from jax.experimental.pallas import tpu as pltpu
from jax.sharding import PartitionSpec as P

HD = 128
UNIT = 8
SPAN = 9
VMEM_BYTES = 63 << 20
SOURCES = (0, 1, 2, 3, 4, 5, 7, 8, 12, 13, 15, 6, 9, 10, 11, 14)
NEAR = 11
PLAN = (
    ("attend", 0, 0), ("attend", 1, 0), ("a", 0, 0), ("attend", 3, 0), ("b", 0, 0), ("a", 3, 0),
    ("b", 0, 2), ("attend", 2, 0), ("b", 0, 1), ("f", 0, 0), ("b", 0, 3), ("a", 1, 0), ("b", 1, 0),
    ("f", 0, 1), ("f", 0, 2), ("near", 0, 0), ("f", 0, 3), ("b", 1, 1), ("b", 1, 2), ("f", 1, 0),
    ("b", 1, 3), ("a", 2, 0), ("done", 0, 0), ("b", 2, 0), ("mm", 0, 0), ("f", 1, 1), ("f", 1, 2),
    ("mm", 0, 1), ("near", 1, 0), ("f", 1, 3), ("b", 2, 1), ("mm", 0, 2), ("b", 2, 2), ("f", 2, 0),
    ("b", 2, 3), ("b", 3, 3), ("done", 1, 0), ("b", 3, 0), ("mm", 1, 0), ("b", 3, 2), ("mm", 1, 1),
    ("b", 3, 1), ("mm", 1, 2), ("mm", 1, 3), ("f", 2, 1), ("f", 2, 2), ("mm", 0, 3), ("f", 2, 3),
    ("near", 2, 0), ("f", 3, 0), ("done", 2, 0), ("f", 3, 1), ("mm", 2, 0), ("mm", 2, 1),
    ("mm", 2, 2), ("f", 3, 3), ("mm", 2, 3), ("f", 3, 2), ("done", 3, 0), ("mm", 3, 0),
    ("mm", 3, 1), ("mm", 3, 2), ("mm", 3, 3),
)
MESH = pl.DeviceIdType.MESH


def kernel(
    lengths_in, units_in, q_ref, k_ref, v_ref, w_ref, out_ref,
    lengths_ref, units_ref, kv_buf, slots, w_buf, q_in, order, out_order, q_rows, pos_buf,
    bias, k_cat, v_cat, att, part_out, part_in, out_tiles, stage,
    load_sem, w_send, w_recv, kv_send, kv_recv, ag_send, ag_recv,
    give_send, give_recv, stage_send, stage_recv, rs_send, rs_recv, out_sem,
):
    ctx, tp, dp = lax.axis_index("ctx"), lax.axis_index("tp"), lax.axis_index("dp")
    y, x = ctx // 4, ctx % 4
    zl, core = tp // 2, tp % 2
    sign = 1 - 2 * core

    def at_plane(yy, xx):
        return {"ctx": ((yy + 4) % 4) * 4 + (xx + 4) % 4}

    def at_z(step):
        moved = zl + step + 4
        return {"tp": (moved % 4) * 2 + core, "dp": (dp + moved // 4 + 3) % 4}

    def at_part(step, c):
        return {"tp": zl * 2 + c, "dp": (dp + step + 4) % 4}

    x_to = (at_plane(y, x + 1), at_plane(y, x - 1), at_plane(y, x + 2))
    y_to = (at_plane(y + 1, x), at_plane(y - 1, x), at_plane(y + 2, x))
    twin = {"tp": zl * 2 + 1 - core}

    barrier = pltpu.get_barrier_semaphore()
    partners = [
        at_part(1, core), at_part(-1, core), at_z(1), at_z(-1), x_to[2], y_to[2],
        *x_to[:2], *y_to[:2], twin,
    ]
    for partner in partners:
        pl.semaphore_signal(barrier, inc=1, device_id=partner, device_id_type=MESH)

    loads = [
        pltpu.make_async_copy(k_ref, kv_buf.at[0, y, x], load_sem.at[0]),
        pltpu.make_async_copy(v_ref, kv_buf.at[1, x, y], load_sem.at[1]),
        pltpu.make_async_copy(units_in, units_ref, load_sem.at[2]),
        pltpu.make_async_copy(lengths_in, lengths_ref, load_sem.at[3]),
        pltpu.make_async_copy(q_ref, q_in, load_sem.at[4]),
        pltpu.make_async_copy(w_ref, w_buf.at[core], load_sem.at[5]),
    ]
    for load in loads:
        load.start()

    offsets = (0, 3, 1, 2)

    def gather_copies(buf, send, recv, direct=()):
        copies = {}
        for half in range(2):
            first, second = (x, y) if half == 0 else (y, x)
            first_to, second_to = (x_to, y_to) if half == 0 else (y_to, x_to)
            regions = []
            for way in range(3):
                regions.append((("a", way), buf.at[half, second, first], first_to[way]))
            for way in range(2):
                line = (second + (3 if way == 0 else 1)) % 4
                for j, offset in enumerate(offsets):
                    place = (first + offset) % 4
                    regions.append((("b", way, j), buf.at[half, second, place], second_to[way]))
                    if j in direct:
                        if way == 0:
                            regions.append((("d", j), buf.at[half, second, place], second_to[2]))
                    else:
                        regions.append((("f", way, j), buf.at[half, line, place, way], second_to[way]))
            for n, (name, region, target) in enumerate(regions):
                copies[(half, *name)] = pltpu.make_async_remote_copy(
                    src_ref=region, dst_ref=region, send_sem=send.at[half, n],
                    recv_sem=recv.at[half, n], device_id=target, device_id_type=MESH,
                )
        return copies

    def e0(g):
        for half in range(2):
            for way in range(2):
                g[half, "a", way].start()
        for half in range(2):
            g[half, "a", 2].start()

    def begin_d(g, j):
        for half in range(2):
            if (half, "d", j) in g:
                g[half, "d", j].start()

    def begin_b(g):
        for half in range(2):
            for way in range(2):
                g[half, "b", way, 0].start()

    def spread(g, way_in, j):
        for half in range(2):
            g[half, "a", way_in].wait_recv()
            for way in range(2):
                g[half, "b", way, j].start()
        begin_d(g, j)

    def forward(g, j):
        for half in range(2):
            for way in range(2):
                g[half, "b", way, j].wait_recv()
                if (half, "f", way, j) in g:
                    g[half, "f", way, j].start()

    def e1(g):
        spread(g, 0, 1)
        spread(g, 1, 2)
        forward(g, 0)

    def e2(g):
        spread(g, 2, 3)

    def e3(g):
        forward(g, 1)
        forward(g, 2)

    def e4(g):
        forward(g, 3)

    def e5(g, wanted=range(4)):
        for name, copy in g.items():
            if (name[1] == "f" and name[3] in wanted) or (name[1] == "d" and name[2] in wanted):
                copy.wait_recv()

    def sent(g):
        for copy in g.values():
            copy.wait_send()

    kv = gather_copies(kv_buf, kv_send, kv_recv, (3,))
    loads[0].wait()
    loads[1].wait()
    pl.semaphore_wait(barrier, len(partners))

    e0(kv)
    begin_b(kv)
    w_copy = pltpu.make_async_remote_copy(
        src_ref=w_ref, dst_ref=w_buf.at[core], send_sem=w_send, recv_sem=w_recv,
        device_id=twin, device_id_type=MESH,
    )
    w_copy.start()
    loads[2].wait()
    loads[3].wait()

    row8 = lax.broadcasted_iota(jnp.int32, (UNIT, HD), 0)
    lane8 = lax.broadcasted_iota(jnp.int32, (UNIT, HD), 1)

    def place(d, carry):
        unit = jnp.zeros((UNIT, HD), jnp.int32)
        for i in range(16):
            value = jnp.full((UNIT, HD), units_ref[d * 16 + i])
            unit = jnp.where(lax.shift_right_logical(value, 4) == ctx, value & 15, unit)
        row = unit * UNIT + row8
        rows = pl.ds(pl.multiple_of(d * UNIT, UNIT), UNIT)
        pos_buf[rows, :] = ctx * 128 + row
        order[rows, :] = (lane8 == row).astype(jnp.float32)
        return carry

    lax.fori_loop(0, 16, place, 0)
    e1(kv)
    e2(kv)
    loads[4].wait()
    ordered = jnp.dot(
        order[...].astype(jnp.bfloat16), q_in[...], preferred_element_type=jnp.float32
    ).astype(jnp.bfloat16)
    for t in range(8):
        for head in range(8):
            q_rows[t, head * 16:(head + 1) * 16, :] = ordered[
                t * 16:(t + 1) * 16, head * HD:(head + 1) * HD
            ]
    pos = pos_buf[...]
    begins = jnp.zeros_like(pos)
    end = jnp.int32(0)
    for j in range(8):
        end = end + lengths_ref[j]
        begins = jnp.where(pos >= end, end, begins)
    lane = lax.broadcasted_iota(jnp.int32, (128, HD), 1)
    for block in range(SPAN):
        key_pos = (ctx - (SPAN - 1) + block) * 128 + lane
        seen = (key_pos >= begins) & (key_pos <= pos)
        bias[:, :, block * 128:(block + 1) * 128] = jnp.where(seen, 0.0, -1e30).reshape(8, 16, HD)
    v_cat[:, HD:] = jnp.ones((SPAN * 128, HD), jnp.bfloat16)
    e3(kv)
    e4(kv)

    def place_out(n, carry):
        source = lax.shift_right_logical(jnp.full((UNIT, HD), units_ref[tp * 32 + n]), 4)
        relative = ((lax.shift_right_logical(source, 2) - y) & 3) * 4 + ((source - x) & 3)
        rank = jnp.zeros((UNIT, HD), jnp.int32)
        for r in range(1, 16):
            rank = jnp.where(relative == SOURCES[r], r, rank)
        row = rank * 16 + (n // 16) * UNIT + row8
        rows = pl.ds(pl.multiple_of(n * UNIT, UNIT), UNIT)
        for side in range(2):
            out_order[rows, side * HD:(side + 1) * HD] = (
                lane8 + side * HD == row
            ).astype(jnp.float32)
        return carry

    lax.fori_loop(0, 32, place_out, 0)
    e5(kv)
    for block in range(SPAN):
        other = (ctx + 16 - (SPAN - 1) + block) % 16
        oy, ox = other // 4, other % 4
        for part in range(2):
            rows = slice(block * 128 + part * 64, block * 128 + part * 64 + 64)
            k_cat[rows, :] = kv_buf[0, oy, ox, part]
            v_cat[rows, :HD] = kv_buf[1, ox, oy, part]

    def swapped(c):
        return zl == 3 * c

    def rows_for(i, c):
        s = 1 - 2 * c
        if i < 2:
            step = jnp.where(swapped(c), (2 * s, -s)[i], (-s, 2 * s)[i])
        else:
            step = (s, 0)[i - 2]
        shifted = zl + step + 4
        return 2 * (shifted % 4) + c, 1 - shifted // 4

    factor = (HD ** -0.5) * 1.4426950408889634

    def attend(k):
        targets = [rows_for(k, c)[0] for c in (core, 1 - core)]
        two = jnp.concatenate([q_rows[t] for t in targets], axis=0)
        scores = lax.dot_general(
            two, k_cat[...], (((1,), (1,)), ((), ())), preferred_element_type=jnp.float32
        ).reshape(2, 8, 16, SPAN * 128)
        masked = jnp.concatenate(
            [scores[n:n + 1] + bias[t][None, None] for n, t in enumerate(targets)], axis=0
        ).reshape(256, SPAN * 128)
        top = jnp.max(masked, axis=1, keepdims=True)
        weights = jnp.exp2((masked - top) * factor).astype(jnp.bfloat16)
        blended = jnp.dot(weights, v_cat[...], preferred_element_type=jnp.float32)
        result = (blended[:, :HD] / blended[:, HD:]).astype(jnp.bfloat16)
        for n, t in enumerate(targets):
            for head in range(8):
                col = (head % 4) * HD
                at = n * 128 + head * 16
                att[t, head // 4, :, col:col + HD] = result[at:at + 16]

    slot_a = jnp.where(core == 0, y, x)
    slot_b = jnp.where(core == 0, x, y)

    slot = (core, slot_a, slot_b)
    other_slot = (1 - core, jnp.where(core == 0, x, y), jnp.where(core == 0, y, x))

    def give_twin(i, relayed):
        t, _ = rows_for(i, 1 - core)
        return pltpu.make_async_remote_copy(
            src_ref=att.at[t], dst_ref=stage.at[i] if relayed else slots.at[i, *slot],
            send_sem=give_send.at[i, 1],
            recv_sem=stage_recv.at[i] if relayed else give_recv.at[i, core],
            device_id=twin, device_id_type=MESH,
        )

    def give_part(i):
        t, ahead = rows_for(i, core)
        return pltpu.make_async_remote_copy(
            src_ref=att.at[t], dst_ref=slots.at[i, *slot],
            send_sem=give_send.at[i, 0], recv_sem=give_recv.at[i, core],
            device_id=at_part(ahead, core), device_id_type=MESH,
        )

    def relay(i):
        _, ahead = rows_for(i, core)
        return pltpu.make_async_remote_copy(
            src_ref=stage.at[i], dst_ref=slots.at[i, *other_slot],
            send_sem=stage_send.at[i], recv_sem=give_recv.at[i, 1 - core],
            device_id=at_part(ahead, core), device_id_type=MESH,
        )

    def give(i):
        if i in (0, 3):
            give_twin(i, False).start()
        else:
            _, twin_ahead = rows_for(i, 1 - core)
            pl.when(twin_ahead == 0)(give_twin(i, False).start)
            pl.when(twin_ahead != 0)(give_twin(i, True).start)
        t, ahead = rows_for(i, core)
        if i in (1, 2):
            pl.when(ahead != 0)(give_part(i).start)

        @pl.when(ahead == 0)
        def _():
            pltpu.make_async_copy(
                att.at[t], slots.at[i, *slot], give_recv.at[i, core]
            ).start()

    def pass_rows(i):
        _, ahead = rows_for(i, core)

        @pl.when(ahead != 0)
        def _():
            pltpu.make_async_copy(att.at[0], stage.at[i], stage_recv.at[i]).wait()
            relay(i).start()

    def given(i):
        give_twin(i, False).wait_send()
        if i in (1, 2):
            _, ahead = rows_for(i, core)
            pl.when(ahead != 0)(give_part(i).wait_send)
            pl.when(ahead != 0)(relay(i).wait_send)

    gathers = [gather_copies(slots.at[k], ag_send.at[k], ag_recv.at[k]) for k in range(4)]

    def start(k):
        for half in range(2):
            pltpu.make_async_copy(
                att.at[0], slots.at[k, half, 0, 0], give_recv.at[k, half]
            ).wait()
        e0(gathers[k])

    groups = (slice(0, NEAR * 16), slice(NEAR * 16, 256))

    def hand_on(k, j, group):
        rows = groups[group]
        return pltpu.make_async_remote_copy(
            src_ref=part_out.at[k, j, rows], dst_ref=part_in.at[k, j, rows],
            send_sem=rs_send.at[k, j, group], recv_sem=rs_recv.at[k, j, group],
            device_id=at_z(jnp.where(k == 0, -sign, sign)), device_id_type=MESH,
        )

    def store(j):
        cols = pl.ds(pl.multiple_of(j * 256, 256), 256)
        return pltpu.make_async_copy(out_tiles.at[j], out_ref.at[:, cols], out_sem.at[j])

    at_y = [(y + d) % 4 for d in range(4)]
    at_x = [(x + d) % 4 for d in range(4)]

    def product(i, j, sources):
        acc = jnp.zeros((len(sources) * 16, 256), jnp.float32)
        for half in range(2):
            for part in range(2):
                left = []
                for n in sources:
                    sy, sx = at_y[n // 4], at_x[n % 4]
                    left.append(slots[i, half, *((sy, sx) if half == 0 else (sx, sy)), part])
                acc = acc + jnp.dot(
                    jnp.concatenate(left, axis=0),
                    w_buf[half, part * 512:(part + 1) * 512, j * 256:(j + 1) * 256],
                    preferred_element_type=jnp.float32,
                )
        return acc

    def pass_on(i, j, group):
        rows = groups[group]
        acc = product(i, j, SOURCES[:NEAR] if group == 0 else SOURCES[NEAR:])
        if i == 2:
            hand_on(1, j, group).wait_recv()
            acc = acc + part_in[1, j, rows].astype(jnp.float32)
        k = 2 if i == 2 else jnp.where(swapped(core), 1 - i, i)
        part_out[k, j, rows] = acc.astype(jnp.bfloat16)
        hand_on(k, j, group).start()

    def finish(j):
        acc = product(3, j, SOURCES)
        for group in range(2):
            hand_on(0, j, group).wait_recv()
            hand_on(2, j, group).wait_recv()
        acc = acc + part_in[0, j].astype(jnp.float32) + part_in[2, j].astype(jnp.float32)
        out_tiles[j] = jnp.dot(
            out_order[...].astype(jnp.bfloat16), acc.astype(jnp.bfloat16),
            preferred_element_type=jnp.float32,
        ).astype(jnp.bfloat16)
        store(j).start()

    def step(op, i, j):
        g = gathers[i]
        if op == "attend":
            attend(i)
            give(i)
        elif op == "a":
            start(i)
        elif op == "b":
            if j == 0:
                begin_b(g)
            else:
                spread(g, j - 1, j)
        elif op == "f":
            forward(g, j)
        elif op == "near":
            e5(g, (0,))
            for n in range(4):
                pass_on(i, n, 0)
        elif op == "done":
            e5(g, range(4) if i == 3 else (1, 2, 3))
        elif i < 3:
            pass_on(i, j, 1)
        else:
            finish(j)

    for op, i, j in PLAN:
        if op == "near" and i == 0:
            w_copy.wait()
            loads[5].wait()
        if op == "done" and i == 3:
            sent(kv)
            for n in range(4):
                given(n)
            for n in range(2):
                sent(gathers[n])
        step(op, i, j)
        if op == "attend" and i == 3:
            pass_rows(1)
        if op == "b" and i == 0 and j == 1:
            pass_rows(2)
    sent(gathers[2])
    sent(gathers[3])
    for k in range(3):
        for j in range(4):
            hand_on(k, j, 0).wait_send()
            hand_on(k, j, 1).wait_send()
    for j in range(4):
        store(j).wait()


def local(queries, key_rows, value_rows, doc_lengths, unit_source, w_out):
    bf16, f32, i32 = jnp.bfloat16, jnp.float32, jnp.int32
    dma = pltpu.SemaphoreType.DMA
    vmem = pltpu.VMEM
    anywhere = pl.BlockSpec(memory_space=pl.ANY)
    return pl.pallas_call(
        kernel,
        out_shape=jax.ShapeDtypeStruct((256, 1024), bf16),
        in_specs=[anywhere] * 6,
        out_specs=anywhere,
        scratch_shapes=[
            pltpu.SMEM((8,), i32),
            pltpu.SMEM((256,), i32),
            vmem((2, 4, 4, 2, 64, HD), bf16),
            vmem((4, 2, 4, 4, 2, 16, 512), bf16),
            vmem((2, 1024, 1024), bf16),
            vmem((128, 1024), bf16),
            vmem((128, HD), f32),
            vmem((256, 256), f32),
            vmem((8, 128, HD), bf16),
            vmem((128, HD), i32),
            vmem((8, 16, SPAN * 128), f32),
            vmem((SPAN * 128, HD), bf16),
            vmem((SPAN * 128, 2 * HD), bf16),
            vmem((8, 2, 16, 512), bf16),
            vmem((3, 4, 256, 256), bf16),
            vmem((3, 4, 256, 256), bf16),
            vmem((4, 256, 256), bf16),
            vmem((4, 2, 16, 512), bf16),
            dma((6,)),
            dma,
            dma,
            dma((2, 19)),
            dma((2, 19)),
            dma((4, 2, 19)),
            dma((4, 2, 19)),
            dma((4, 2)),
            dma((4, 2)),
            dma((4,)),
            dma((4,)),
            dma((3, 4, 2)),
            dma((3, 4, 2)),
            dma((4,)),
        ],
        compiler_params=pltpu.CompilerParams(
            collective_id=0, has_side_effects=True, vmem_limit_bytes=VMEM_BYTES
        ),
        cost_estimate=pl.CostEstimate(
            flops=5_500_000_000, bytes_accessed=8_000_000, transcendentals=1_200_000
        ),
    )(
        doc_lengths, unit_source, queries,
        key_rows.reshape(2, 64, HD), value_rows.reshape(2, 64, HD), w_out,
    )


def solution(mesh):
    return jax.shard_map(
        local,
        mesh=mesh,
        in_specs=(
            P(("dp", "ctx"), "tp"),
            P(("dp", "ctx"), "tp"),
            P(("dp", "ctx"), "tp"),
            P("dp"),
            P("dp"),
            P("tp", "ctx"),
        ),
        out_specs=P(("dp", "tp"), "ctx"),
        check_vma=False,
    )
```
